32 devices in a mesh: grp: 2 (over y), seq: 4 (over z), rep: 2 (over x), sub: 2 (over core).
Axes of the slice: x: 2, y: 2, z: 4, core: 2. Of those that a mesh axis runs over, the one named last changes fastest.
Arguments:
- prompt_q: bfloat16 [1024, 512], P(('grp', 'seq', 'rep'), 'sub'), parts along dimension 0, may hold values from -16 to 16
- prompt_kv: bfloat16 [1024, 256], P(('grp', 'seq', 'rep')), parts along dimension 0, may hold values from -6 to 6
- prompt_dout: bfloat16 [1024, 512], P(('grp', 'seq', 'rep'), 'sub'), parts along dimension 0, may hold values from -6 to 6
- resp_q: bfloat16 [8, 256, 512], P(('grp', 'rep', 'sub'), 'seq'), parts along dimension 0, may hold values from -16 to 16
- resp_kv: bfloat16 [8, 256, 256], P(('grp', 'rep', 'sub'), 'seq'), parts along dimension 0, may hold values from -6 to 6
- resp_dout: bfloat16 [8, 256, 512], P(('grp', 'rep', 'sub'), 'seq'), parts along dimension 0, may hold values from -6 to 6
- resp_lengths: int32 [8], P('grp'), parts along dimension 0, may hold values from 1 to 256, 640 in all
Outputs:
- prompt_out: bfloat16 [1024, 512], P(('grp', 'seq', 'rep'), 'sub'), parts along dimension 0
- resp_out: bfloat16 [8, 256, 512], P(('grp', 'rep', 'sub'), 'seq'), parts along dimension 0
- prompt_dq: bfloat16 [1024, 512], P(('grp', 'seq', 'rep'), 'sub'), parts along dimension 0
- resp_dq: bfloat16 [8, 256, 512], P(('grp', 'rep', 'sub'), 'seq'), parts along dimension 0
- prompt_dkv: bfloat16 [1024, 256], P(('grp', 'seq', 'rep')), parts along dimension 0
- resp_dkv: bfloat16 [8, 256, 256], P(('grp', 'rep', 'sub'), 'seq'), parts along dimension 0
The draws below stay inside these ranges and needn't reach their ends.
There are 2 independent parts, one for each index of `grp`. The reference program is written for one: setup_inputs(seed, part) draws one part's arguments, and reference() takes and returns one part's arrays. A program takes and returns all parts, laid end to end along the dimension named above; each array names one. Nothing has to cross between parts.
Inputs may be any that keep to these rules, and one draw needn't show every extreme that they name: `resp_lengths`: the lengths sum to 640; the largest is 256.
All inputs are finite; a program needn't handle non-finite values.
Results may differ from the reference program's by a relative error of at most 0.0093.
Values may be sent and summed in bfloat16 or wider, within the bound.
A program may use at most 128 MiB of HBM per device.

```python
import math
import jax
import jax.numpy as jnp
import numpy as np
from jax import lax

HEADS = 4
E = 128
LR_DEV = 64
P_SIZE = 512
L_MAX = 256
RESP = 4
RESP_TOTAL = 640
N_SEQ = 4


def draw_prompt_kv(key, part):
    key = jax.random.fold_in(key, 1)
    values = jnp.clip(jax.random.normal(key, (P_SIZE, 2 * E), jnp.float32), -6.0, 6.0)
    return values.astype(jnp.bfloat16)


def draw_prompt_q(key, part):
    key = jax.random.fold_in(key, 2)
    values = jnp.clip(jax.random.normal(key, (P_SIZE, HEADS * E), jnp.float32), -6.0, 6.0)
    return values.astype(jnp.bfloat16)


def draw_resp_q(key, part):
    key = jax.random.fold_in(key, 3)
    values = jnp.clip(jax.random.normal(key, (RESP, L_MAX, HEADS * E), jnp.float32), -6.0, 6.0)
    return values.astype(jnp.bfloat16)


def levels(own_key, dims, shards, least, high):
    factor_of = 1.0
    for axis_at, parts in shards:
        steps = jax.random.uniform(jax.random.fold_in(jax.random.fold_in(own_key, 6), axis_at), (parts,), jnp.float32, least / len(shards), high / len(shards))
        factor_of = factor_of * jnp.repeat(jnp.exp(steps), dims[axis_at] // parts).reshape((-1,) + (1,) * (len(dims) - 1 - axis_at))
    return factor_of


def split_up(amount, total, reach, slope):
    weights = [(1 << 20) // math.isqrt(grade ** slope) + 1 for grade in range(2, amount + 1)]
    rest, holding = total - reach - (amount - 1), [1] * (amount - 1)
    while rest > 0:
        free = [i for i in range(amount - 1) if holding[i] < reach]
        pool, remaining = sum([weights[i] for i in free]), rest
        for i in free:
            addition = min(reach - holding[i], max(1, remaining * weights[i] // pool), rest)
            holding[i] = holding[i] + addition
            rest = rest - addition
    return np.array([reach] + holding)


def uneven_parts(own_key, amount, total, most, slope):
    if amount == 2:
        one = jax.random.randint(own_key, (), max(1, total - most), min(most, total - 1) + 1)
        return jnp.stack([one, total - one])
    tallies = jnp.asarray(split_up(amount, total, most, slope), jnp.int32)
    couples = (amount - 1) // 2
    source_of, sink = tallies[1:1 + 2 * couples:2], tallies[2:2 + 2 * couples:2]
    room = jnp.minimum(source_of - 1, most - sink)
    moved = jax.random.randint(jax.random.fold_in(own_key, 1), (couples,), 0, 1 << 20) % (room + 1)
    tallies = tallies.at[1:1 + 2 * couples:2].set(source_of - moved).at[2:2 + 2 * couples:2].set(sink + moved)
    return tallies[jax.random.permutation(jax.random.fold_in(own_key, 2), amount)]


def gaussian(own_key, shape, spread, most, shards=(), kind=jnp.bfloat16):
    entries = jax.random.normal(own_key, shape, jnp.float32) * spread
    if len(shards) > 0:
        entries = levels(own_key, shape, shards, -0.22, 0.18) * entries
    return jnp.clip(entries, min=-most, max=most).astype(kind)


def setup_inputs(seed: int = 0, part: int = 0) -> dict:
    keys = jax.random.split(jax.random.key(seed), 8)
    part_keys = jax.random.split(jax.random.fold_in(keys[7], part), 8)
    return {
        "prompt_q": draw_prompt_q(jax.random.fold_in(jax.random.fold_in(keys[7], part), 71), part),
        "prompt_kv": draw_prompt_kv(jax.random.fold_in(jax.random.fold_in(keys[7], part), 71), part),
        "prompt_dout": gaussian(part_keys[2], (P_SIZE, HEADS * E), 1.0, 6.0, ((0, 8), (1, 2))),
        "resp_q": draw_resp_q(jax.random.fold_in(jax.random.fold_in(keys[7], part), 71), part),
        "resp_kv": gaussian(part_keys[4], (RESP, L_MAX, 2 * E), 1.0, 6.0, ((0, 4), (1, 4))),
        "resp_dout": gaussian(part_keys[5], (RESP, L_MAX, HEADS * E), 1.0, 6.0, ((0, 4), (1, 4))),
        "resp_lengths": uneven_parts(part_keys[6], RESP, RESP_TOTAL, L_MAX, 2).astype(jnp.int32),
    }


def to_half(values):
    rounded = values.astype(jnp.bfloat16)
    rounded = lax.optimization_barrier(rounded)
    return rounded.astype(jnp.float32)

def attend(queries, cotangent, key_array, key_pos, query_pos, live_rows):
    head_dim = key_array.shape[1] // 2
    score_scale = 1.0 / math.sqrt(head_dim)
    query_f32 = queries.astype(jnp.float32)
    cotan_f32 = cotangent.astype(jnp.float32)
    key_f32 = key_array[:, :head_dim].astype(jnp.float32)
    value_f32 = key_array[:, head_dim:].astype(jnp.float32)
    scores = jnp.einsum('qhe,ke->hqk', query_f32, key_f32) * score_scale
    allowed = (key_pos[None, :] <= query_pos[:, None])[None]
    row_top = lax.optimization_barrier(jnp.max(jnp.where(allowed, scores, -jnp.inf), axis=2, keepdims=True))
    exp_scores = jnp.where(allowed, jnp.exp(scores - row_top), 0.0)
    prob_f32 = exp_scores / lax.optimization_barrier(jnp.sum(exp_scores, axis=2, keepdims=True))
    keep_rows = live_rows.astype(jnp.float32)[None, :, None]
    weights = to_half(prob_f32) * keep_rows
    output = jnp.einsum('hqk,ke->qhe', weights, value_f32)
    grad_prob = jnp.einsum('qhe,ke->hqk', cotan_f32, value_f32)
    row_delta = jnp.transpose(lax.optimization_barrier(jnp.sum(cotan_f32 * output, axis=2)))
    dscore = to_half(prob_f32 * (grad_prob - row_delta[:, :, None])) * keep_rows
    dquery = jnp.einsum('hqk,ke->qhe', dscore, key_f32) * score_scale
    key_grad = jnp.einsum('hqk,qhe->ke', dscore, query_f32) * score_scale
    dvalue = jnp.einsum('hqk,qhe->ke', weights, cotan_f32)
    return (output, dquery, jnp.concatenate([key_grad, dvalue], axis=1))

def reference(prompt_q, prompt_kv, prompt_dout, resp_q, resp_kv, resp_dout, resp_lengths):
    prompt_pos = jnp.arange(P_SIZE, dtype=jnp.int32)
    block_rows = P_SIZE // N_SEQ

    def prompt_step(grad_sum, block_index):
        first_row = block_index * block_rows
        query_block = lax.dynamic_slice_in_dim(prompt_q, first_row, block_rows, 0).reshape(block_rows, HEADS, E)
        cotan_block = lax.dynamic_slice_in_dim(prompt_dout, first_row, block_rows, 0).reshape(block_rows, HEADS, E)
        query_pos = first_row + jnp.arange(block_rows, dtype=jnp.int32)
        output, dquery, key_grads = attend(query_block, cotan_block, prompt_kv, prompt_pos, query_pos, jnp.ones((block_rows,), jnp.int32))
        return (grad_sum + key_grads, (output.reshape(block_rows, HEADS * E), dquery.reshape(block_rows, HEADS * E)))
    prompt_grad, (prompt_output, prompt_dquery) = lax.scan(prompt_step, jnp.zeros((P_SIZE, 2 * E), jnp.float32), jnp.arange(N_SEQ, dtype=jnp.int32))
    prompt_output = prompt_output.reshape(P_SIZE, HEADS * E)
    prompt_dquery = prompt_dquery.reshape(P_SIZE, HEADS * E)
    joined_pos = jnp.arange(P_SIZE + L_MAX, dtype=jnp.int32)

    def response(grad_sum, resp_item):
        queries, cotangent, own_keys, length = resp_item
        joined = jnp.concatenate([prompt_kv, own_keys], axis=0)

        def block(key_total, block_index):
            first_row = block_index * LR_DEV
            query_block = lax.dynamic_slice_in_dim(queries, first_row, LR_DEV, 0).reshape(LR_DEV, HEADS, E)
            cotan_block = lax.dynamic_slice_in_dim(cotangent, first_row, LR_DEV, 0).reshape(LR_DEV, HEADS, E)
            positions = first_row + jnp.arange(LR_DEV, dtype=jnp.int32)
            output, dquery, key_grads = attend(query_block, cotan_block, joined, joined_pos, P_SIZE + positions, positions < length)
            return (key_total + key_grads, (output.reshape(LR_DEV, HEADS * E), dquery.reshape(LR_DEV, HEADS * E)))
        key_total, (output, dquery) = lax.scan(block, jnp.zeros((P_SIZE + L_MAX, 2 * E), jnp.float32), jnp.arange(N_SEQ, dtype=jnp.int32))
        return (grad_sum + key_total[:P_SIZE], (output.reshape(L_MAX, HEADS * E), dquery.reshape(L_MAX, HEADS * E), key_total[P_SIZE:]))
    prompt_grad, (resp_output, resp_dquery, resp_grad) = lax.scan(response, prompt_grad, (resp_q, resp_dout, resp_kv, resp_lengths))
    return (prompt_output.astype(jnp.bfloat16), resp_output.astype(jnp.bfloat16), prompt_dquery.astype(jnp.bfloat16), resp_dquery.astype(jnp.bfloat16), prompt_grad.astype(jnp.bfloat16), resp_grad.astype(jnp.bfloat16))
```

```python
import functools
import math

import jax
import jax.numpy as jnp
from jax import lax
from jax.experimental import pallas as pl
from jax.experimental.pallas import tpu as pltpu
from jax.sharding import PartitionSpec as P

MESH = pl.DeviceIdType.MESH
NT = (((1,), (1,)), ((), ()))
NN = (((1,), (0,)), ((), ()))
TN = (((0,), (0,)), ((), ()))
floor_score = -1e30
f32, bf16 = jnp.float32, jnp.bfloat16


def dot(a, b, dims):
    return lax.dot_general(a, b, dims, preferred_element_type=f32)


def loop(low, high, body):
    if high - low <= 8:
        for i in range(low, high):
            body(i)
    else:
        lax.fori_loop(low, high, lambda i, c: (body(i), c)[1], 0)


def fold(count, body, carry):
    if count <= 4:
        for i in range(count):
            carry = body(i, carry)
        return carry
    return lax.fori_loop(0, count, body, carry)


def kernel(
    nz, nx, ns, lens, pq, pkv, pdo, rq, rkv, rdo, po, ro, pdq, rdq, pdkv, rdkv,
    pk, rk, qa, da, sp, gp, so, go, wp, dp, wo, do, away, got, mine, rs, oway, rr, fin,
    g_send, g_recv, f_send, f_recv, r_send, r_recv, p_sem, s_send, s_recv, q_send, q_recv, e_sem,
):
    n = nz * nx
    rows, kvw = pkv.shape
    e = kvw // 2
    half = rows // 2
    z, x, h = lax.axis_index("seq"), lax.axis_index("rep"), lax.axis_index("sub")
    me = z * nx + x
    sib = {"sub": 1 - h}
    p_heads = pq.shape[1] // e
    r_heads = rq.shape[2] // e
    r_rows = rq.shape[1]
    rc = r_heads * r_rows
    pc = p_heads * rows
    scale = 1.0 / math.sqrt(e)
    scale2 = scale * math.log2(math.e)
    bk = sp.shape[1]
    cpb = bk // half
    nb2 = sp.shape[0]
    nb = nb2 // 2
    bo = so.shape[1]
    zpb = bo // r_rows
    no = so.shape[0]

    def chip(c):
        return {"seq": c // nx, "rep": c % nx}

    def copy(src, dst, send, recv, to):
        return pltpu.make_async_remote_copy(
            src_ref=src, dst_ref=dst, send_sem=send, recv_sem=recv, device_id=to, device_id_type=MESH
        )

    barrier = pltpu.get_barrier_semaphore()

    def greet(d):
        pl.semaphore_signal(barrier, inc=1, device_id=chip((me + d) % n), device_id_type=MESH)

    loop(1, n, greet)
    pl.semaphore_signal(barrier, inc=1, device_id=sib, device_id_type=MESH)

    for k in range(2):
        pk[k * n + me] = pkv[k * half : (k + 1) * half, :]
    rk[z] = rkv[0]

    def blank(i):
        @pl.when(i > z)
        def _():
            rk[i] = jnp.zeros(rk.shape[1:], bf16)

    loop(0, nz, blank)
    for k in range(r_heads):
        qa[k * r_rows : (k + 1) * r_rows, :] = rq[0, :, k * e : (k + 1) * e]
        da[k * r_rows : (k + 1) * r_rows, :] = rdo[0, :, k * e : (k + 1) * e]
    for k in range(p_heads):
        qa[rc + k * rows : rc + (k + 1) * rows, :] = pq[:, k * e : (k + 1) * e]
        da[rc + k * rows : rc + (k + 1) * rows, :] = pdo[:, k * e : (k + 1) * e]

    pl.semaphore_wait(barrier, n)

    def gather(c, src):
        return copy(pk.at[h * n + src], pk.at[h * n + src], g_send.at[c], g_recv.at[src], chip(c))

    def pass_on(c, k):
        return copy(pk.at[k * n + c], pk.at[k * n + c], f_send.at[c], f_recv.at[c], sib)

    def resp(to, src):
        return copy(rk.at[src], rk.at[src], r_send.at[to], r_recv.at[src], {"seq": to})

    loop(1, n, lambda d: gather((me + d) % n, me).start())

    def resp_start(i):
        @pl.when(i > z)
        def _():
            resp(i, z).start()

    loop(0, nz, resp_start)

    def forward(d):
        c = (me + n - d) % n
        gather(c, c).wait_recv()
        pass_on(c, h).start()

    loop(1, n, forward)

    def resp_wait(i):
        @pl.when(i < z)
        def _():
            resp(i, i).wait_recv()

    loop(0, nz, resp_wait)

    def own_scores(i, top):
        kv = rk[pl.ds(i * zpb, zpb)].reshape(bo, kvw)
        s = dot(kv[:, :e], qa[:rc], NT) * scale2
        key = i * bo + lax.broadcasted_iota(jnp.int32, (bo, rc), 0)
        at = z * r_rows + lax.broadcasted_iota(jnp.int32, (bo, rc), 1) % r_rows
        s = jnp.where(key <= at, s, floor_score)
        so[i] = s
        go[i] = dot(kv[:, e:], da[:rc], NT)
        return jnp.maximum(top, jnp.max(s, axis=0, keepdims=True))

    top_r = fold(no, own_scores, jnp.full((1, rc), floor_score, f32))

    loop(1, n, lambda d: pass_on((me + d) % n, 1 - h).wait_recv())

    def scores(i, tops):
        top_r, top_p = tops
        kv = pk[pl.ds(i * cpb, cpb)].reshape(bk, kvw)
        s = dot(kv[:, :e], qa[...], NT) * scale2
        place = lax.broadcasted_iota(jnp.int32, (bk, pc), 0)
        key = ((i % nb) * cpb + place // half) * rows + (i // nb) * half + place % half
        at = me * rows + lax.broadcasted_iota(jnp.int32, (bk, pc), 1) % rows
        s_r = s[:, :rc]
        s_p = jnp.where(key <= at, s[:, rc:], floor_score)
        sp[i, :, :rc] = s_r
        sp[i, :, rc:] = s_p
        gp[i] = dot(kv[:, e:], da[...], NT)
        return (
            jnp.maximum(top_r, jnp.max(s_r, axis=0, keepdims=True)),
            jnp.maximum(top_p, jnp.max(s_p, axis=0, keepdims=True)),
        )

    top_r, top_p = fold(nb2, scores, (top_r, jnp.full((1, pc), floor_score, f32)))
    top = jnp.concatenate([top_r, top_p], axis=1)

    def own_exp(i, sums):
        total, delta = sums
        ex = jnp.exp2(so[i] - top_r)
        so[i] = ex
        return (
            total + jnp.sum(ex, axis=0, keepdims=True),
            delta + jnp.sum(ex * go[i], axis=0, keepdims=True),
        )

    def all_exp(i, sums):
        total, delta = sums
        ex = jnp.exp2(sp[i] - top)
        sp[i] = ex
        return (
            total + jnp.sum(ex, axis=0, keepdims=True),
            delta + jnp.sum(ex * gp[i], axis=0, keepdims=True),
        )

    zero_r, zero_a = jnp.zeros((1, rc), f32), jnp.zeros((1, rc + pc), f32)
    total_o, delta_o = fold(no, own_exp, (zero_r, zero_r))
    total, delta = fold(nb2, all_exp, (zero_a, zero_a))
    total_r = total[:, :rc] + total_o
    total = jnp.concatenate([total_r, total[:, rc:]], axis=1)
    delta = jnp.concatenate([delta[:, :rc] + delta_o, delta[:, rc:]], axis=1) / total
    length = lens[x * ns + h]
    column = lax.broadcasted_iota(jnp.int32, (1, rc + pc), 1)
    live = jnp.logical_or(column >= rc, z * r_rows + column % r_rows < length)
    share = jnp.where(live, 1.0 / total, 0.0)

    def weigh(i, carry):
        prob = sp[i] * share
        wp[i] = prob.astype(bf16)
        dp[i] = (prob * (gp[i] - delta)).astype(bf16)
        return carry

    def own_weigh(i, carry):
        prob = so[i] * share[:, :rc]
        wo[i] = prob.astype(bf16)
        do[i] = (prob * (go[i] - delta[:, :rc])).astype(bf16)
        return carry

    fold(nb2, weigh, 0)
    fold(no, own_weigh, 0)

    def part(k, b):
        dk = dot(dp[k * nb + b], qa[...], NN) * scale
        dv = dot(wp[k * nb + b], da[...], NN)
        return jnp.concatenate([dk, dv], axis=1)

    def sib_part(b, carry):
        away[b] = part(1 - h, b).astype(bf16)
        return carry

    fold(nb, sib_part, 0)
    pair = copy(away, got, p_sem.at[0], p_sem.at[1], sib)
    pair.start()

    def own_part(i, carry):
        dk = dot(do[i], qa[:rc], NN) * scale
        dv = dot(wo[i], da[:rc], NN)
        both = jnp.concatenate([dk, dv], axis=1).astype(bf16)
        oway[pl.ds(i * zpb, zpb)] = both.reshape(zpb, r_rows, kvw)
        return carry

    fold(no, own_part, 0)

    def back(to, src):
        return copy(oway.at[to], rr.at[src], q_send.at[to], q_recv.at[src], {"seq": to})

    def back_start(i):
        @pl.when(i < z)
        def _():
            back(i, z).start()

    loop(0, nz, back_start)

    def my_part(b, carry):
        mine[b] = part(h, b)
        return carry

    fold(nb, my_part, 0)
    pair.wait_recv()

    def add(b, carry):
        both = (mine[b] + got[b].astype(f32)).astype(bf16)
        rs[0, pl.ds(b * cpb, cpb)] = both.reshape(cpb, half, kvw)
        return carry

    fold(nb, add, 0)

    def scatter(c, src):
        return copy(rs.at[0, c], rs.at[1, src], s_send.at[c], s_recv.at[src], chip(c))

    loop(1, n, lambda d: scatter((me + d) % n, me).start())
    rs[1, me] = rs[0, me]

    def out_own(i, carry):
        o, q = carry
        kv = rk[pl.ds(i * zpb, zpb)].reshape(bo, kvw)
        return o + dot(kv[:, e:], wo[i], TN), q + dot(kv[:, :e], do[i], TN)

    def out_all(i, carry):
        o, q = carry
        kv = pk[pl.ds(i * cpb, cpb)].reshape(bk, kvw)
        return o + dot(kv[:, e:], wp[i], TN), q + dot(kv[:, :e], dp[i], TN)

    zo, za = jnp.zeros((e, rc), f32), jnp.zeros((e, rc + pc), f32)
    o_o, q_o = fold(no, out_own, (zo, zo))
    o_a, q_a = fold(nb2, out_all, (za, za))
    o_r = jnp.transpose(o_a[:, :rc] + o_o)
    o_p = jnp.transpose(o_a[:, rc:])
    q_r = jnp.transpose((q_a[:, :rc] + q_o) * scale)
    q_p = jnp.transpose(q_a[:, rc:] * scale)
    for k in range(r_heads):
        ro[0, :, k * e : (k + 1) * e] = o_r[k * r_rows : (k + 1) * r_rows].astype(bf16)
        rdq[0, :, k * e : (k + 1) * e] = q_r[k * r_rows : (k + 1) * r_rows].astype(bf16)
    for k in range(p_heads):
        po[:, k * e : (k + 1) * e] = o_p[k * rows : (k + 1) * rows].astype(bf16)
        pdq[:, k * e : (k + 1) * e] = q_p[k * rows : (k + 1) * rows].astype(bf16)

    loop(1, n, lambda d: scatter((me + n - d) % n, (me + n - d) % n).wait_recv())
    summed = lax.fori_loop(
        0, n, lambda c, t: t + rs[1, c].astype(f32), jnp.zeros((half, kvw), f32), unroll=min(n, 8)
    )
    fin[h] = summed.astype(bf16)
    last = copy(fin.at[h], fin.at[h], e_sem.at[0], e_sem.at[1], sib)
    last.start()

    def back_wait(i):
        @pl.when(i > z)
        def _():
            back(i, i).wait_recv()

    loop(0, nz, back_wait)
    rr[z] = oway[z]
    own_sum = lax.fori_loop(
        0,
        nz,
        lambda c, t: t + jnp.where(c >= z, rr[c].astype(f32), 0.0),
        jnp.zeros((r_rows, kvw), f32),
        unroll=min(nz, 8),
    )
    rdkv[0] = own_sum.astype(bf16)
    copy(fin.at[1 - h], fin.at[1 - h], e_sem.at[0], e_sem.at[1], sib).wait_recv()
    pdkv[:half, :] = fin[0]
    pdkv[half:, :] = fin[1]

    loop(1, n, lambda d: gather((me + d) % n, me).wait_send())
    loop(1, n, lambda d: pass_on((me + d) % n, h).wait_send())
    loop(1, n, lambda d: scatter((me + d) % n, me).wait_send())

    def sent(i):
        @pl.when(i > z)
        def _():
            resp(i, z).wait_send()

        @pl.when(i < z)
        def _():
            back(i, z).wait_send()

    loop(0, nz, sent)
    pair.wait_send()
    last.wait_send()


def shards(nz, nx, ns, prompt_q, prompt_kv, prompt_dout, resp_q, resp_kv, resp_dout, resp_lengths):
    n = nz * nx
    rows, kvw = prompt_kv.shape
    e = kvw // 2
    half = rows // 2
    r_rows = resp_q.shape[1]
    rc = resp_q.shape[2] // e * r_rows
    qc = rc + prompt_q.shape[1] // e * rows
    cpb = math.gcd(n, 8)
    bk = cpb * half
    nb2 = 2 * n // cpb
    zpb = math.gcd(nz, 4)
    bo = zpb * r_rows
    no = nz // zpb
    vmem = pl.BlockSpec(memory_space=pltpu.VMEM)
    scratch = [
        ((2 * n, half, kvw), bf16),
        ((nz, r_rows, kvw), bf16),
        ((qc, e), bf16),
        ((qc, e), bf16),
        ((nb2, bk, qc), f32),
        ((nb2, bk, qc), f32),
        ((no, bo, rc), f32),
        ((no, bo, rc), f32),
        ((nb2, bk, qc), bf16),
        ((nb2, bk, qc), bf16),
        ((no, bo, rc), bf16),
        ((no, bo, rc), bf16),
        ((nb2 // 2, bk, kvw), bf16),
        ((nb2 // 2, bk, kvw), bf16),
        ((nb2 // 2, bk, kvw), f32),
        ((2, n, half, kvw), bf16),
        ((nz, r_rows, kvw), bf16),
        ((nz, r_rows, kvw), bf16),
        ((2, half, kvw), bf16),
    ]
    room = sum(math.prod(s) * jnp.dtype(t).itemsize for s, t in scratch)
    dma = pltpu.SemaphoreType.DMA
    sems = [dma((k,)) for k in (n, n, n, n, nz, nz, 2, n, n, nz, nz, 2)]
    like = jax.ShapeDtypeStruct
    return pl.pallas_call(
        functools.partial(kernel, nz, nx, ns),
        out_shape=[
            like(a.shape, bf16)
            for a in (prompt_q, resp_q, prompt_q, resp_q, prompt_kv, resp_kv)
        ],
        in_specs=[pl.BlockSpec(memory_space=pltpu.SMEM)] + [vmem] * 6,
        out_specs=[vmem] * 6,
        scratch_shapes=[pltpu.VMEM(s, t) for s, t in scratch] + sems,
        compiler_params=pltpu.CompilerParams(
            collective_id=0, has_side_effects=True, vmem_limit_bytes=room + 8 * 2**20
        ),
    )(resp_lengths, prompt_q, prompt_kv, prompt_dout, resp_q, resp_kv, resp_dout)


def solution(mesh):
    prompt = P(("grp", "seq", "rep"), "sub")
    prompt_kv = P(("grp", "seq", "rep"), None)
    resp = P(("grp", "rep", "sub"), "seq", None)
    sizes = (mesh.shape["seq"], mesh.shape["rep"], mesh.shape["sub"])
    return jax.shard_map(
        functools.partial(shards, *sizes),
        mesh=mesh,
        in_specs=(prompt, prompt_kv, prompt, resp, resp, resp, P("grp")),
        out_specs=(prompt, resp, prompt, resp, prompt_kv, resp),
        check_vma=False,
    )
```

```python
import functools
import math

import jax
import jax.numpy as jnp
from jax import lax
from jax.experimental import pallas as pl
from jax.experimental.pallas import tpu as pltpu
from jax.sharding import PartitionSpec as P

MESH = pl.DeviceIdType.MESH
NT = (((1,), (1,)), ((), ()))
NN = (((1,), (0,)), ((), ()))
TN = (((0,), (0,)), ((), ()))
floor_score = -1e30
f32, bf16 = jnp.float32, jnp.bfloat16


def dot(a, b, dims):
    return lax.dot_general(a, b, dims, preferred_element_type=f32)


def loop(low, high, body):
    if high - low <= 8:
        for i in range(low, high):
            body(i)
    else:
        lax.fori_loop(low, high, lambda i, c: (body(i), c)[1], 0)


def fold(count, body, carry):
    if count <= 4:
        for i in range(count):
            carry = body(i, carry)
        return carry
    return lax.fori_loop(0, count, body, carry)


def kernel(
    nz, nx, ns, lens_in, pq, pkv, pdo, rq, rkv, rdo, po, ro, pdq, rdq, pdkv, rdkv,
    pk, rk, qa, da, sp, gp, so, go, wp, dp, wo, do, away, got, mine, rs, oway, rr, fin, lens, in_sem,
    g_send, g_recv, f_send, f_recv, r_send, r_recv, p_sem, s_send, s_recv, q_send, q_recv, e_sem,
):
    n = nz * nx
    rows, kvw = pkv.shape
    e = kvw // 2
    half = rows // 2
    z, x, h = lax.axis_index("seq"), lax.axis_index("rep"), lax.axis_index("sub")
    me = z * nx + x
    sib = {"sub": 1 - h}
    p_heads = pq.shape[1] // e
    r_heads = rq.shape[2] // e
    r_rows = rq.shape[1]
    rc = r_heads * r_rows
    pc = p_heads * rows
    scale = 1.0 / math.sqrt(e)
    scale2 = scale * math.log2(math.e)
    bk = sp.shape[1]
    cpb = bk // half
    nb2 = sp.shape[0]
    nb = nb2 // 2
    bo = so.shape[1]
    zpb = bo // r_rows
    no = so.shape[0]

    def chip(c):
        return {"seq": c // nx, "rep": c % nx}

    def copy(src, dst, send, recv, to):
        return pltpu.make_async_remote_copy(
            src_ref=src, dst_ref=dst, send_sem=send, recv_sem=recv, device_id=to, device_id_type=MESH
        )

    barrier = pltpu.get_barrier_semaphore()

    def greet(d):
        pl.semaphore_signal(barrier, inc=1, device_id=chip((me + d) % n), device_id_type=MESH)

    loop(1, n, greet)
    pl.semaphore_signal(barrier, inc=1, device_id=sib, device_id_type=MESH)

    moves = [(pkv.at[k * half : (k + 1) * half], pk.at[k * n + me]) for k in range(2)]
    moves += [(rkv.at[0], rk.at[z])]
    for to, resp_in, prompt_in in ((qa, rq, pq), (da, rdo, pdo)):
        for k in range(r_heads):
            moves.append((resp_in.at[0, :, k * e : (k + 1) * e], to.at[k * r_rows : (k + 1) * r_rows]))
        for k in range(p_heads):
            first = rc + k * rows
            moves.append((prompt_in.at[:, k * e : (k + 1) * e], to.at[first : first + rows]))
    moves.append((lens_in, lens))
    moves = [pltpu.make_async_copy(a, b, in_sem.at[k]) for k, (a, b) in enumerate(moves)]
    for move in moves:
        move.start()

    def blank(i):
        @pl.when(i > z)
        def _():
            rk[i] = jnp.zeros(rk.shape[1:], bf16)

    loop(0, nz, blank)

    pl.semaphore_wait(barrier, n)

    def gather(c, src):
        return copy(pkv.at[pl.ds(pl.multiple_of(h * half, half), half)], pk.at[h * n + src], g_send.at[c], g_recv.at[src], chip(c))

    def pass_on(c, k):
        return copy(pk.at[k * n + c], pk.at[k * n + c], f_send.at[c], f_recv.at[c], sib)

    def resp(to, src):
        return copy(rkv.at[0], rk.at[src], r_send.at[to], r_recv.at[src], {"seq": to})

    loop(1, n, lambda d: gather((me + d) % n, me).start())

    def resp_start(i):
        @pl.when(i > z)
        def _():
            resp(i, z).start()

    loop(0, nz, resp_start)
    for move in moves:
        move.wait()

    def forward(d):
        c = (me + n - d) % n
        gather(c, c).wait_recv()
        pass_on(c, h).start()

    loop(1, n, forward)

    def resp_wait(i):
        @pl.when(i < z)
        def _():
            resp(i, i).wait_recv()

    loop(0, nz, resp_wait)

    def own_scores(i, top):
        kv = rk[pl.ds(i * zpb, zpb)].reshape(bo, kvw)
        s = dot(kv[:, :e], qa[:rc], NT) * scale2
        key = i * bo + lax.broadcasted_iota(jnp.int32, (bo, rc), 0)
        at = z * r_rows + lax.broadcasted_iota(jnp.int32, (bo, rc), 1) % r_rows
        s = jnp.where(key <= at, s, floor_score)
        so[i] = s
        go[i] = dot(kv[:, e:], da[:rc], NT)
        return jnp.maximum(top, jnp.max(s, axis=0, keepdims=True))

    top_r = fold(no, own_scores, jnp.full((1, rc), floor_score, f32))

    loop(1, n, lambda d: pass_on((me + d) % n, 1 - h).wait_recv())

    def scores(i, tops):
        top_r, top_p = tops
        kv = pk[pl.ds(i * cpb, cpb)].reshape(bk, kvw)
        s = dot(kv[:, :e], qa[...], NT) * scale2
        place = lax.broadcasted_iota(jnp.int32, (bk, pc), 0)
        key = ((i % nb) * cpb + place // half) * rows + (i // nb) * half + place % half
        at = me * rows + lax.broadcasted_iota(jnp.int32, (bk, pc), 1) % rows
        s_r = s[:, :rc]
        s_p = jnp.where(key <= at, s[:, rc:], floor_score)
        sp[i, :, :rc] = s_r
        sp[i, :, rc:] = s_p
        gp[i] = dot(kv[:, e:], da[...], NT).astype(gp.dtype)
        return (
            jnp.maximum(top_r, jnp.max(s_r, axis=0, keepdims=True)),
            jnp.maximum(top_p, jnp.max(s_p, axis=0, keepdims=True)),
        )

    top_r, top_p = fold(nb2, scores, (top_r, jnp.full((1, pc), floor_score, f32)))
    top = jnp.concatenate([top_r, top_p], axis=1)

    def own_exp(i, sums):
        total, delta = sums
        ex = jnp.exp2(so[i] - top_r)
        so[i] = ex
        return (
            total + jnp.sum(ex, axis=0, keepdims=True),
            delta + jnp.sum(ex * go[i], axis=0, keepdims=True),
        )

    def all_exp(i, sums):
        total, delta = sums
        ex = jnp.exp2(sp[i] - top)
        sp[i] = ex
        return (
            total + jnp.sum(ex, axis=0, keepdims=True),
            delta + jnp.sum(ex * gp[i].astype(f32), axis=0, keepdims=True),
        )

    zero_r, zero_a = jnp.zeros((1, rc), f32), jnp.zeros((1, rc + pc), f32)
    total_o, delta_o = fold(no, own_exp, (zero_r, zero_r))
    total, delta = fold(nb2, all_exp, (zero_a, zero_a))
    total_r = total[:, :rc] + total_o
    total = jnp.concatenate([total_r, total[:, rc:]], axis=1)
    delta = jnp.concatenate([delta[:, :rc] + delta_o, delta[:, rc:]], axis=1) / total
    length = lens[x * ns + h]
    column = lax.broadcasted_iota(jnp.int32, (1, rc + pc), 1)
    live = jnp.logical_or(column >= rc, z * r_rows + column % r_rows < length)
    share = jnp.where(live, 1.0 / total, 0.0)

    def weigh(i, carry):
        prob = sp[i] * share
        wp[i] = prob.astype(bf16)
        dp[i] = (prob * (gp[i].astype(f32) - delta)).astype(bf16)
        return carry

    def own_weigh(i, carry):
        prob = so[i] * share[:, :rc]
        wo[i] = prob.astype(bf16)
        do[i] = (prob * (go[i] - delta[:, :rc])).astype(bf16)
        return carry

    fold(nb2, weigh, 0)
    fold(no, own_weigh, 0)

    def part(k, b):
        dk = dot(dp[k * nb + b], qa[...], NN) * scale
        dv = dot(wp[k * nb + b], da[...], NN)
        return jnp.concatenate([dk, dv], axis=1)

    def sib_part(b, carry):
        away[b] = part(1 - h, b).astype(bf16)
        return carry

    fold(nb, sib_part, 0)
    pair = copy(away, got, p_sem.at[0], p_sem.at[1], sib)
    pair.start()

    def own_part(i, carry):
        dk = dot(do[i], qa[:rc], NN) * scale
        dv = dot(wo[i], da[:rc], NN)
        both = jnp.concatenate([dk, dv], axis=1).astype(bf16)
        oway[pl.ds(i * zpb, zpb)] = both.reshape(zpb, r_rows, kvw)
        return carry

    fold(no, own_part, 0)

    def back(to, src):
        return copy(oway.at[to], rr.at[src], q_send.at[to], q_recv.at[src], {"seq": to})

    def back_start(i):
        @pl.when(i < z)
        def _():
            back(i, z).start()

    loop(0, nz, back_start)

    def my_part(b, carry):
        mine[b] = part(h, b)
        return carry

    fold(nb, my_part, 0)
    pair.wait_recv()

    def add(b, carry):
        both = (mine[b] + got[b].astype(f32)).astype(bf16)
        rs[0, pl.ds(b * cpb, cpb)] = both.reshape(cpb, half, kvw)
        return carry

    fold(nb, add, 0)

    def scatter(c, src):
        return copy(rs.at[0, c], rs.at[1, src], s_send.at[c], s_recv.at[src], chip(c))

    loop(1, n, lambda d: scatter((me + d) % n, me).start())
    rs[1, me] = rs[0, me]

    def out_own(i, carry):
        o, q = carry
        kv = rk[pl.ds(i * zpb, zpb)].reshape(bo, kvw)
        return o + dot(kv[:, e:], wo[i], TN), q + dot(kv[:, :e], do[i], TN)

    def out_all(i, carry):
        o, q = carry
        kv = pk[pl.ds(i * cpb, cpb)].reshape(bk, kvw)
        return o + dot(kv[:, e:], wp[i], TN), q + dot(kv[:, :e], dp[i], TN)

    zo, za = jnp.zeros((e, rc), f32), jnp.zeros((e, rc + pc), f32)
    o_o, q_o = fold(no, out_own, (zo, zo))
    o_a, q_a = fold(nb2, out_all, (za, za))
    o_r = jnp.transpose(o_a[:, :rc] + o_o)
    o_p = jnp.transpose(o_a[:, rc:])
    q_r = jnp.transpose((q_a[:, :rc] + q_o) * scale)
    q_p = jnp.transpose(q_a[:, rc:] * scale)
    for k in range(r_heads):
        ro[0, :, k * e : (k + 1) * e] = o_r[k * r_rows : (k + 1) * r_rows].astype(bf16)
        rdq[0, :, k * e : (k + 1) * e] = q_r[k * r_rows : (k + 1) * r_rows].astype(bf16)
    for k in range(p_heads):
        po[:, k * e : (k + 1) * e] = o_p[k * rows : (k + 1) * rows].astype(bf16)
        pdq[:, k * e : (k + 1) * e] = q_p[k * rows : (k + 1) * rows].astype(bf16)

    loop(1, n, lambda d: scatter((me + n - d) % n, (me + n - d) % n).wait_recv())
    summed = lax.fori_loop(
        0, n, lambda c, t: t + rs[1, c].astype(f32), jnp.zeros((half, kvw), f32), unroll=min(n, 8)
    )
    fin[h] = summed.astype(bf16)
    last = copy(fin.at[h], fin.at[h], e_sem.at[0], e_sem.at[1], sib)
    last.start()

    def back_wait(i):
        @pl.when(i > z)
        def _():
            back(i, i).wait_recv()

    loop(0, nz, back_wait)
    rr[z] = oway[z]
    own_sum = lax.fori_loop(
        0,
        nz,
        lambda c, t: t + jnp.where(c >= z, rr[c].astype(f32), 0.0),
        jnp.zeros((r_rows, kvw), f32),
        unroll=min(nz, 8),
    )
    rdkv[0] = own_sum.astype(bf16)
    copy(fin.at[1 - h], fin.at[1 - h], e_sem.at[0], e_sem.at[1], sib).wait_recv()
    pdkv[:half, :] = fin[0]
    pdkv[half:, :] = fin[1]

    loop(1, n, lambda d: gather((me + d) % n, me).wait_send())
    loop(1, n, lambda d: pass_on((me + d) % n, h).wait_send())
    loop(1, n, lambda d: scatter((me + d) % n, me).wait_send())

    def sent(i):
        @pl.when(i > z)
        def _():
            resp(i, z).wait_send()

        @pl.when(i < z)
        def _():
            back(i, z).wait_send()

    loop(0, nz, sent)
    pair.wait_send()
    last.wait_send()


def hand_over(*refs):
    sem = refs[-1]
    half = len(refs) // 2
    moves = [pltpu.make_async_copy(refs[k], refs[half + k], sem.at[k]) for k in range(half)]
    for move in moves:
        move.start()
    for move in moves:
        move.wait()


def shards(nz, nx, ns, prompt_q, prompt_kv, prompt_dout, resp_q, resp_kv, resp_dout, resp_lengths):
    n = nz * nx
    rows, kvw = prompt_kv.shape
    e = kvw // 2
    half = rows // 2
    r_rows = resp_q.shape[1]
    rc = resp_q.shape[2] // e * r_rows
    qc = rc + prompt_q.shape[1] // e * rows
    cpb = math.gcd(n, 8)
    bk = cpb * half
    nb2 = 2 * n // cpb
    zpb = math.gcd(nz, 4)
    bo = zpb * r_rows
    no = nz // zpb
    vmem = pl.BlockSpec(memory_space=pltpu.VMEM)
    scratch = [
        ((2 * n, half, kvw), bf16),
        ((nz, r_rows, kvw), bf16),
        ((qc, e), bf16),
        ((qc, e), bf16),
        ((nb2, bk, qc), f32),
        ((nb2, bk, qc), f32 if n <= 32 else bf16),
        ((no, bo, rc), f32),
        ((no, bo, rc), f32),
        ((nb2, bk, qc), bf16),
        ((nb2, bk, qc), bf16),
        ((no, bo, rc), bf16),
        ((no, bo, rc), bf16),
        ((nb2 // 2, bk, kvw), bf16),
        ((nb2 // 2, bk, kvw), bf16),
        ((nb2 // 2, bk, kvw), f32),
        ((2, n, half, kvw), bf16),
        ((nz, r_rows, kvw), bf16),
        ((nz, r_rows, kvw), bf16),
        ((2, half, kvw), bf16),
    ]
    room = sum(math.prod(s) * jnp.dtype(t).itemsize for s, t in scratch)
    dma = pltpu.SemaphoreType.DMA
    heads = qc // rows
    sems = [pltpu.SMEM(resp_lengths.shape, jnp.int32)]
    sems += [dma((k,)) for k in (2 * heads + 4, n, n, n, n, nz, nz, 2, n, n, nz, nz, 2)]
    like = jax.ShapeDtypeStruct
    results = pl.pallas_call(
        functools.partial(kernel, nz, nx, ns),
        out_shape=[
            pltpu.VMEM(a.shape, bf16)
            for a in (prompt_q, resp_q, prompt_q, resp_q, prompt_kv, resp_kv)
        ],
        in_specs=[pl.BlockSpec(memory_space=pltpu.HBM)] * 7,
        out_specs=[vmem] * 6,
        scratch_shapes=[pltpu.VMEM(s, t) for s, t in scratch] + sems,
        compiler_params=pltpu.CompilerParams(
            collective_id=0, has_side_effects=True, vmem_limit_bytes=max(56 * 2**20, room + 3 * 2**20)
        ),
    )(resp_lengths, prompt_q, prompt_kv, prompt_dout, resp_q, resp_kv, resp_dout)
    return pl.pallas_call(
        hand_over,
        out_shape=[like(a.shape, a.dtype) for a in results],
        in_specs=[pl.BlockSpec(memory_space=pl.ANY)] * 6,
        out_specs=[pl.BlockSpec(memory_space=pltpu.HBM)] * 6,
        scratch_shapes=[dma((6,))],
    )(*results)


def solution(mesh):
    prompt = P(("grp", "seq", "rep"), "sub")
    prompt_kv = P(("grp", "seq", "rep"), None)
    resp = P(("grp", "rep", "sub"), "seq", None)
    sizes = (mesh.shape["seq"], mesh.shape["rep"], mesh.shape["sub"])
    return jax.shard_map(
        functools.partial(shards, *sizes),
        mesh=mesh,
        in_specs=(prompt, prompt_kv, prompt, resp, resp, resp, P("grp")),
        out_specs=(prompt, resp, prompt, resp, prompt_kv, resp),
        check_vma=False,
    )
```

```python
import functools
import math

import jax
import jax.numpy as jnp
from jax import lax
from jax.experimental import pallas as pl
from jax.experimental.pallas import tpu as pltpu
from jax.sharding import PartitionSpec as P

MESH = pl.DeviceIdType.MESH
NT = (((1,), (1,)), ((), ()))
NN = (((1,), (0,)), ((), ()))
TN = (((0,), (0,)), ((), ()))
floor_score = -1e30
f32, bf16 = jnp.float32, jnp.bfloat16


def dot(a, b, dims):
    return lax.dot_general(a, b, dims, preferred_element_type=f32)


def loop(low, high, body):
    if high - low <= 8:
        for i in range(low, high):
            body(i)
    else:
        lax.fori_loop(low, high, lambda i, c: (body(i), c)[1], 0)


def fold(count, body, carry):
    if count <= 4:
        for i in range(count):
            carry = body(i, carry)
        return carry
    return lax.fori_loop(0, count, body, carry)


def kernel(
    nz, nx, ns, lens_in, pq, pkv, pdo, rq, rkv, rdo, po, ro, pdq, rdq, pdkv, rdkv,
    pk, rk, qa, da, sp, gp, so, go, wp, dp, wo, do, away, got, mine, rs, oway, rr, fin, lens, in_sem,
    g_send, g_recv, f_send, f_recv, r_send, r_recv, p_sem, s_send, s_recv, q_send, q_recv, e_sem,
):
    n = nz * nx
    rows, kvw = pkv.shape
    e = kvw // 2
    half = rows // 2
    z, x, h = lax.axis_index("seq"), lax.axis_index("rep"), lax.axis_index("sub")
    me = z * nx + x
    sib = {"sub": 1 - h}
    p_heads = pq.shape[1] // e
    r_heads = rq.shape[2] // e
    r_rows = rq.shape[1]
    rc = r_heads * r_rows
    pc = p_heads * rows
    scale = 1.0 / math.sqrt(e)
    scale2 = scale * math.log2(math.e)
    bk = sp.shape[1]
    cpb = bk // half
    nb2 = sp.shape[0]
    nb = nb2 // 2
    bo = so.shape[1]
    zpb = bo // r_rows
    no = so.shape[0]

    def chip(c):
        return {"seq": c // nx, "rep": c % nx}

    def copy(src, dst, send, recv, to):
        return pltpu.make_async_remote_copy(
            src_ref=src, dst_ref=dst, send_sem=send, recv_sem=recv, device_id=to, device_id_type=MESH
        )

    barrier = pltpu.get_barrier_semaphore()

    def greet(d):
        pl.semaphore_signal(barrier, inc=1, device_id=chip((me + d) % n), device_id_type=MESH)

    loop(1, n, greet)
    pl.semaphore_signal(barrier, inc=1, device_id=sib, device_id_type=MESH)

    moves = [(pkv.at[k * half : (k + 1) * half], pk.at[k * n + me]) for k in range(2)]
    moves += [(rkv.at[0], rk.at[z])]
    for to, resp_in, prompt_in in ((qa, rq, pq), (da, rdo, pdo)):
        for k in range(r_heads):
            moves.append((resp_in.at[0, :, k * e : (k + 1) * e], to.at[k * r_rows : (k + 1) * r_rows]))
        for k in range(p_heads):
            first = rc + k * rows
            moves.append((prompt_in.at[:, k * e : (k + 1) * e], to.at[first : first + rows]))
    moves.append((lens_in, lens))
    moves = [pltpu.make_async_copy(a, b, in_sem.at[k]) for k, (a, b) in enumerate(moves)]
    for move in moves:
        move.start()

    def blank(i):
        @pl.when(i > z)
        def _():
            rk[i] = jnp.zeros(rk.shape[1:], bf16)

    loop(0, nz, blank)

    pl.semaphore_wait(barrier, n)

    def gather(c, src):
        return copy(pkv.at[pl.ds(pl.multiple_of(h * half, half), half)], pk.at[h * n + src], g_send.at[c], g_recv.at[src], chip(c))

    def pass_on(c, k):
        return copy(pk.at[k * n + c], pk.at[k * n + c], f_send.at[c], f_recv.at[c], sib)

    def resp(to, src):
        return copy(rkv.at[0], rk.at[src], r_send.at[to], r_recv.at[src], {"seq": to})

    loop(1, n, lambda d: gather((me + d) % n, me).start())

    def resp_start(i):
        @pl.when(i > z)
        def _():
            resp(i, z).start()

    loop(0, nz, resp_start)
    for move in moves:
        move.wait()

    def forward(d):
        c = (me + n - d) % n
        gather(c, c).wait_recv()
        pass_on(c, h).start()

    loop(1, n, forward)

    def resp_wait(i):
        @pl.when(i < z)
        def _():
            resp(i, i).wait_recv()

    loop(0, nz, resp_wait)

    def own_scores(i, top):
        kv = rk[pl.ds(i * zpb, zpb)].reshape(bo, kvw)
        s = dot(kv[:, :e], qa[:rc], NT) * scale2
        key = i * bo + lax.broadcasted_iota(jnp.int32, (bo, rc), 0)
        at = z * r_rows + lax.broadcasted_iota(jnp.int32, (bo, rc), 1) % r_rows
        s = jnp.where(key <= at, s, floor_score)
        so[i] = s
        go[i] = dot(kv[:, e:], da[:rc], NT)
        return jnp.maximum(top, jnp.max(s, axis=0, keepdims=True))

    top_r = fold(no, own_scores, jnp.full((1, rc), floor_score, f32))

    loop(1, n, lambda d: pass_on((me + d) % n, 1 - h).wait_recv())

    def scores(i, tops):
        top_r, top_p = tops
        kv = pk[pl.ds(i * cpb, cpb)].reshape(bk, kvw)
        s = dot(kv[:, :e], qa[...], NT) * scale2
        place = lax.broadcasted_iota(jnp.int32, (bk, pc), 0)
        key = ((i % nb) * cpb + place // half) * rows + (i // nb) * half + place % half
        at = me * rows + lax.broadcasted_iota(jnp.int32, (bk, pc), 1) % rows
        s_r = s[:, :rc]
        s_p = jnp.where(key <= at, s[:, rc:], floor_score)
        sp[i, :, :rc] = s_r
        sp[i, :, rc:] = s_p
        gp[i] = dot(kv[:, e:], da[...], NT).astype(gp.dtype)
        return (
            jnp.maximum(top_r, jnp.max(s_r, axis=0, keepdims=True)),
            jnp.maximum(top_p, jnp.max(s_p, axis=0, keepdims=True)),
        )

    top_r, top_p = fold(nb2, scores, (top_r, jnp.full((1, pc), floor_score, f32)))
    top = jnp.concatenate([top_r, top_p], axis=1)

    def own_exp(i, sums):
        total, delta = sums
        ex = jnp.exp2(so[i] - top_r)
        so[i] = ex
        return (
            total + jnp.sum(ex, axis=0, keepdims=True),
            delta + jnp.sum(ex * go[i], axis=0, keepdims=True),
        )

    def all_exp(i, sums):
        total, delta = sums
        ex = jnp.exp2(sp[i] - top)
        sp[i] = ex
        return (
            total + jnp.sum(ex, axis=0, keepdims=True),
            delta + jnp.sum(ex * gp[i].astype(f32), axis=0, keepdims=True),
        )

    zero_r, zero_a = jnp.zeros((1, rc), f32), jnp.zeros((1, rc + pc), f32)
    total_o, delta_o = fold(no, own_exp, (zero_r, zero_r))
    total, delta = fold(nb2, all_exp, (zero_a, zero_a))
    total_r = total[:, :rc] + total_o
    total = jnp.concatenate([total_r, total[:, rc:]], axis=1)
    delta = jnp.concatenate([delta[:, :rc] + delta_o, delta[:, rc:]], axis=1) / total
    length = lens[x * ns + h]
    column = lax.broadcasted_iota(jnp.int32, (1, rc + pc), 1)
    live = jnp.logical_or(column >= rc, z * r_rows + column % r_rows < length)
    share = jnp.where(live, 1.0 / total, 0.0)

    def weigh(i, carry):
        prob = sp[i] * share
        wp[i] = prob.astype(bf16)
        dp[i] = (prob * (gp[i].astype(f32) - delta)).astype(bf16)
        return carry

    def own_weigh(i, carry):
        prob = so[i] * share[:, :rc]
        wo[i] = prob.astype(bf16)
        do[i] = (prob * (go[i] - delta[:, :rc])).astype(bf16)
        return carry

    fold(nb2, weigh, 0)
    fold(no, own_weigh, 0)

    def part(k, b):
        dk = dot(dp[k * nb + b], qa[...], NN) * scale
        dv = dot(wp[k * nb + b], da[...], NN)
        return jnp.concatenate([dk, dv], axis=1)

    def sib_part(b, carry):
        away[b] = part(1 - h, b).astype(bf16)
        return carry

    fold(nb, sib_part, 0)
    pair = copy(away, got, p_sem.at[0], p_sem.at[1], sib)
    pair.start()

    def own_part(i, carry):
        dk = dot(do[i], qa[:rc], NN) * scale
        dv = dot(wo[i], da[:rc], NN)
        both = jnp.concatenate([dk, dv], axis=1).astype(bf16)
        oway[pl.ds(i * zpb, zpb)] = both.reshape(zpb, r_rows, kvw)
        return carry

    fold(no, own_part, 0)

    def back(to, src):
        return copy(oway.at[to], rr.at[src], q_send.at[to], q_recv.at[src], {"seq": to})

    def back_start(i):
        @pl.when(i < z)
        def _():
            back(i, z).start()


    def my_part(b, carry):
        mine[b] = part(h, b)
        return carry

    fold(nb, my_part, 0)
    pair.wait_recv()

    def add(b, carry):
        both = (mine[b] + got[b].astype(f32)).astype(bf16)
        rs[0, pl.ds(b * cpb, cpb)] = both.reshape(cpb, half, kvw)
        return carry

    fold(nb, add, 0)

    def scatter(c, src):
        return copy(rs.at[0, c], rs.at[1, src], s_send.at[c], s_recv.at[src], chip(c))

    loop(1, n, lambda d: scatter((me + d) % n, me).start())
    loop(0, nz, back_start)
    rs[1, me] = rs[0, me]

    def out_own(i, carry):
        o, q = carry
        kv = rk[pl.ds(i * zpb, zpb)].reshape(bo, kvw)
        return o + dot(kv[:, e:], wo[i], TN), q + dot(kv[:, :e], do[i], TN)

    def out_all(i, carry):
        o, q = carry
        kv = pk[pl.ds(i * cpb, cpb)].reshape(bk, kvw)
        return o + dot(kv[:, e:], wp[i], TN), q + dot(kv[:, :e], dp[i], TN)

    zo, za = jnp.zeros((e, rc), f32), jnp.zeros((e, rc + pc), f32)
    o_o, q_o = fold(no, out_own, (zo, zo))
    o_a, q_a = fold(nb2, out_all, (za, za))
    o_r = jnp.transpose(o_a[:, :rc] + o_o)
    o_p = jnp.transpose(o_a[:, rc:])
    q_r = jnp.transpose((q_a[:, :rc] + q_o) * scale)
    q_p = jnp.transpose(q_a[:, rc:] * scale)
    for k in range(r_heads):
        ro[0, :, k * e : (k + 1) * e] = o_r[k * r_rows : (k + 1) * r_rows].astype(bf16)
        rdq[0, :, k * e : (k + 1) * e] = q_r[k * r_rows : (k + 1) * r_rows].astype(bf16)
    for k in range(p_heads):
        po[:, k * e : (k + 1) * e] = o_p[k * rows : (k + 1) * rows].astype(bf16)
        pdq[:, k * e : (k + 1) * e] = q_p[k * rows : (k + 1) * rows].astype(bf16)

    loop(1, n, lambda d: scatter((me + n - d) % n, (me + n - d) % n).wait_recv())
    summed = lax.fori_loop(
        0, n, lambda c, t: t + rs[1, c].astype(f32), jnp.zeros((half, kvw), f32), unroll=min(n, 8)
    )
    fin[h] = summed.astype(bf16)
    last = copy(fin.at[h], fin.at[h], e_sem.at[0], e_sem.at[1], sib)
    last.start()

    def back_wait(i):
        @pl.when(i > z)
        def _():
            back(i, i).wait_recv()

    loop(0, nz, back_wait)
    rr[z] = oway[z]
    own_sum = lax.fori_loop(
        0,
        nz,
        lambda c, t: t + jnp.where(c >= z, rr[c].astype(f32), 0.0),
        jnp.zeros((r_rows, kvw), f32),
        unroll=min(nz, 8),
    )
    rdkv[0] = own_sum.astype(bf16)
    copy(fin.at[1 - h], fin.at[1 - h], e_sem.at[0], e_sem.at[1], sib).wait_recv()
    pdkv[:half, :] = fin[0]
    pdkv[half:, :] = fin[1]

    loop(1, n, lambda d: gather((me + d) % n, me).wait_send())
    loop(1, n, lambda d: pass_on((me + d) % n, h).wait_send())
    loop(1, n, lambda d: scatter((me + d) % n, me).wait_send())

    def sent(i):
        @pl.when(i > z)
        def _():
            resp(i, z).wait_send()

        @pl.when(i < z)
        def _():
            back(i, z).wait_send()

    loop(0, nz, sent)
    pair.wait_send()
    last.wait_send()


def hand_over(*refs):
    sem = refs[-1]
    half = len(refs) // 2
    moves = [pltpu.make_async_copy(refs[k], refs[half + k], sem.at[k]) for k in range(half)]
    for move in moves:
        move.start()
    for move in moves:
        move.wait()


def shards(nz, nx, ns, prompt_q, prompt_kv, prompt_dout, resp_q, resp_kv, resp_dout, resp_lengths):
    n = nz * nx
    rows, kvw = prompt_kv.shape
    e = kvw // 2
    half = rows // 2
    r_rows = resp_q.shape[1]
    rc = resp_q.shape[2] // e * r_rows
    qc = rc + prompt_q.shape[1] // e * rows
    cpb = math.gcd(n, 8)
    bk = cpb * half
    nb2 = 2 * n // cpb
    zpb = math.gcd(nz, 4)
    bo = zpb * r_rows
    no = nz // zpb
    vmem = pl.BlockSpec(memory_space=pltpu.VMEM)
    scratch = [
        ((2 * n, half, kvw), bf16),
        ((nz, r_rows, kvw), bf16),
        ((qc, e), bf16),
        ((qc, e), bf16),
        ((nb2, bk, qc), f32),
        ((nb2, bk, qc), f32 if n <= 32 else bf16),
        ((no, bo, rc), f32),
        ((no, bo, rc), f32),
        ((nb2, bk, qc), bf16),
        ((nb2, bk, qc), bf16),
        ((no, bo, rc), bf16),
        ((no, bo, rc), bf16),
        ((nb2 // 2, bk, kvw), bf16),
        ((nb2 // 2, bk, kvw), bf16),
        ((nb2 // 2, bk, kvw), f32),
        ((2, n, half, kvw), bf16),
        ((nz, r_rows, kvw), bf16),
        ((nz, r_rows, kvw), bf16),
        ((2, half, kvw), bf16),
    ]
    room = sum(math.prod(s) * jnp.dtype(t).itemsize for s, t in scratch)
    dma = pltpu.SemaphoreType.DMA
    heads = qc // rows
    sems = [pltpu.SMEM(resp_lengths.shape, jnp.int32)]
    sems += [dma((k,)) for k in (2 * heads + 4, n, n, n, n, nz, nz, 2, n, n, nz, nz, 2)]
    like = jax.ShapeDtypeStruct
    results = pl.pallas_call(
        functools.partial(kernel, nz, nx, ns),
        out_shape=[
            pltpu.VMEM(a.shape, bf16)
            for a in (prompt_q, resp_q, prompt_q, resp_q, prompt_kv, resp_kv)
        ],
        in_specs=[pl.BlockSpec(memory_space=pltpu.HBM)] * 7,
        out_specs=[vmem] * 6,
        scratch_shapes=[pltpu.VMEM(s, t) for s, t in scratch] + sems,
        compiler_params=pltpu.CompilerParams(
            collective_id=0, has_side_effects=True, vmem_limit_bytes=max(56 * 2**20, room + 3 * 2**20)
        ),
    )(resp_lengths, prompt_q, prompt_kv, prompt_dout, resp_q, resp_kv, resp_dout)
    return pl.pallas_call(
        hand_over,
        out_shape=[like(a.shape, a.dtype) for a in results],
        in_specs=[vmem] * 6,
        out_specs=[pl.BlockSpec(memory_space=pltpu.HBM)] * 6,
        scratch_shapes=[dma((6,))],
        compiler_params=pltpu.CompilerParams(vmem_limit_bytes=4 * 2**20),
    )(*results)


def solution(mesh):
    prompt = P(("grp", "seq", "rep"), "sub")
    prompt_kv = P(("grp", "seq", "rep"), None)
    resp = P(("grp", "rep", "sub"), "seq", None)
    sizes = (mesh.shape["seq"], mesh.shape["rep"], mesh.shape["sub"])
    return jax.shard_map(
        functools.partial(shards, *sizes),
        mesh=mesh,
        in_specs=(prompt, prompt_kv, prompt, resp, resp, resp, P("grp")),
        out_specs=(prompt, resp, prompt, resp, prompt_kv, resp),
        check_vma=False,
    )
```

```python
import functools
import math

import jax
import jax.numpy as jnp
from jax import lax
from jax.experimental import pallas as pl
from jax.experimental.pallas import tpu as pltpu
from jax.sharding import PartitionSpec as P

MESH = pl.DeviceIdType.MESH
NT = (((1,), (1,)), ((), ()))
NN = (((1,), (0,)), ((), ()))
TN = (((0,), (0,)), ((), ()))
floor_score = -1e30
f32, bf16 = jnp.float32, jnp.bfloat16


def dot(a, b, dims):
    return lax.dot_general(a, b, dims, preferred_element_type=f32)


def loop(low, high, body):
    if high - low <= 8:
        for i in range(low, high):
            body(i)
    else:
        lax.fori_loop(low, high, lambda i, c: (body(i), c)[1], 0)


def fold(count, body, carry):
    if count <= 4:
        for i in range(count):
            carry = body(i, carry)
        return carry
    return lax.fori_loop(0, count, body, carry)


def kernel(
    nz, nx, ns, lens_in, pq, pkv, pdo, rq, rkv, rdo, po, ro, pdq, rdq, pdkv, rdkv,
    pk, rk, qa, da, sp, gp, so, go, wp, dp, wo, do, away, got, mine, rs, oway, rr, fin, lens, in_sem,
    g_send, g_recv, f_send, f_recv, r_send, r_recv, p_sem, s_send, s_recv, q_send, q_recv, e_sem,
):
    n = nz * nx
    rows, kvw = pkv.shape
    e = kvw // 2
    half = rows // 2
    z, x, h = lax.axis_index("seq"), lax.axis_index("rep"), lax.axis_index("sub")
    me = z * nx + x
    sib = {"sub": 1 - h}
    p_heads = pq.shape[1] // e
    r_heads = rq.shape[2] // e
    r_rows = rq.shape[1]
    rc = r_heads * r_rows
    pc = p_heads * rows
    scale = 1.0 / math.sqrt(e)
    scale2 = scale * math.log2(math.e)
    bk = sp.shape[1]
    cpb = bk // half
    nb2 = sp.shape[0]
    nb = nb2 // 2
    bo = so.shape[1]
    zpb = bo // r_rows
    no = so.shape[0]

    def chip(c):
        return {"seq": c // nx, "rep": c % nx}

    def copy(src, dst, send, recv, to):
        return pltpu.make_async_remote_copy(
            src_ref=src, dst_ref=dst, send_sem=send, recv_sem=recv, device_id=to, device_id_type=MESH
        )

    barrier = pltpu.get_barrier_semaphore()

    def greet(d):
        pl.semaphore_signal(barrier, inc=1, device_id=chip((me + d) % n), device_id_type=MESH)

    loop(1, n, greet)
    pl.semaphore_signal(barrier, inc=1, device_id=sib, device_id_type=MESH)

    moves = [(pkv.at[k * half : (k + 1) * half], pk.at[k * n + me]) for k in range(2)]
    moves += [(rkv.at[0], rk.at[z])]
    for to, resp_in, prompt_in in ((qa, rq, pq), (da, rdo, pdo)):
        for k in range(r_heads):
            moves.append((resp_in.at[0, :, k * e : (k + 1) * e], to.at[k * r_rows : (k + 1) * r_rows]))
        for k in range(p_heads):
            first = rc + k * rows
            moves.append((prompt_in.at[:, k * e : (k + 1) * e], to.at[first : first + rows]))
    moves.append((lens_in, lens))
    moves = [pltpu.make_async_copy(a, b, in_sem.at[k]) for k, (a, b) in enumerate(moves)]
    for move in moves:
        move.start()

    def blank(i):
        @pl.when(i > z)
        def _():
            rk[i] = jnp.zeros(rk.shape[1:], bf16)

    loop(0, nz, blank)

    pl.semaphore_wait(barrier, n)

    def gather(c, src):
        return copy(pkv.at[pl.ds(pl.multiple_of(h * half, half), half)], pk.at[h * n + src], g_send.at[c], g_recv.at[src], chip(c))

    def pass_on(c, k):
        return copy(pk.at[k * n + c], pk.at[k * n + c], f_send.at[c], f_recv.at[c], sib)

    def resp(to, src):
        return copy(rkv.at[0], rk.at[src], r_send.at[to], r_recv.at[src], {"seq": to})

    loop(1, n, lambda d: gather((me + d) % n, me).start())

    def resp_start(i):
        @pl.when(i > z)
        def _():
            resp(i, z).start()

    loop(0, nz, resp_start)
    for move in moves:
        move.wait()

    def forward(d):
        c = (me + n - d) % n
        gather(c, c).wait_recv()
        pass_on(c, h).start()

    loop(1, n, forward)

    loop(1, n, lambda d: pass_on((me + d) % n, 1 - h).wait_recv())

    def scores(i, tops):
        top_r, top_p = tops
        kv = pk[pl.ds(i * cpb, cpb)].reshape(bk, kvw)
        s = dot(kv[:, :e], qa[...], NT) * scale2
        place = lax.broadcasted_iota(jnp.int32, (bk, pc), 0)
        key = ((i % nb) * cpb + place // half) * rows + (i // nb) * half + place % half
        at = me * rows + lax.broadcasted_iota(jnp.int32, (bk, pc), 1) % rows
        s_r = s[:, :rc]
        s_p = jnp.where(key <= at, s[:, rc:], floor_score)
        sp[i, :, :rc] = s_r
        sp[i, :, rc:] = s_p
        gp[i] = dot(kv[:, e:], da[...], NT).astype(gp.dtype)
        return (
            jnp.maximum(top_r, jnp.max(s_r, axis=0, keepdims=True)),
            jnp.maximum(top_p, jnp.max(s_p, axis=0, keepdims=True)),
        )

    top_r, top_p = fold(nb2, scores, (jnp.full((1, rc), floor_score, f32), jnp.full((1, pc), floor_score, f32)))
    def resp_wait(i):
        @pl.when(i < z)
        def _():
            resp(i, i).wait_recv()

    loop(0, nz, resp_wait)

    def own_scores(i, top):
        kv = rk[pl.ds(i * zpb, zpb)].reshape(bo, kvw)
        s = dot(kv[:, :e], qa[:rc], NT) * scale2
        key = i * bo + lax.broadcasted_iota(jnp.int32, (bo, rc), 0)
        at = z * r_rows + lax.broadcasted_iota(jnp.int32, (bo, rc), 1) % r_rows
        s = jnp.where(key <= at, s, floor_score)
        so[i] = s
        go[i] = dot(kv[:, e:], da[:rc], NT)
        return jnp.maximum(top, jnp.max(s, axis=0, keepdims=True))

    top_r = fold(no, own_scores, top_r)

    top = jnp.concatenate([top_r, top_p], axis=1)

    def own_exp(i, sums):
        total, delta = sums
        ex = jnp.exp2(so[i] - top_r)
        so[i] = ex
        return (
            total + jnp.sum(ex, axis=0, keepdims=True),
            delta + jnp.sum(ex * go[i], axis=0, keepdims=True),
        )

    def all_exp(i, sums):
        total, delta = sums
        ex = jnp.exp2(sp[i] - top)
        sp[i] = ex
        return (
            total + jnp.sum(ex, axis=0, keepdims=True),
            delta + jnp.sum(ex * gp[i].astype(f32), axis=0, keepdims=True),
        )

    zero_r, zero_a = jnp.zeros((1, rc), f32), jnp.zeros((1, rc + pc), f32)
    total_o, delta_o = fold(no, own_exp, (zero_r, zero_r))
    total, delta = fold(nb2, all_exp, (zero_a, zero_a))
    total_r = total[:, :rc] + total_o
    total = jnp.concatenate([total_r, total[:, rc:]], axis=1)
    delta = jnp.concatenate([delta[:, :rc] + delta_o, delta[:, rc:]], axis=1) / total
    length = lens[x * ns + h]
    column = lax.broadcasted_iota(jnp.int32, (1, rc + pc), 1)
    live = jnp.logical_or(column >= rc, z * r_rows + column % r_rows < length)
    share = jnp.where(live, 1.0 / total, 0.0)

    def weigh(i, carry):
        prob = sp[i] * share
        wp[i] = prob.astype(bf16)
        dp[i] = (prob * (gp[i].astype(f32) - delta)).astype(bf16)
        return carry

    def own_weigh(i, carry):
        prob = so[i] * share[:, :rc]
        wo[i] = prob.astype(bf16)
        do[i] = (prob * (go[i] - delta[:, :rc])).astype(bf16)
        return carry

    fold(nb2, weigh, 0)
    fold(no, own_weigh, 0)

    def part(k, b):
        dk = dot(dp[k * nb + b], qa[...], NN) * scale
        dv = dot(wp[k * nb + b], da[...], NN)
        return jnp.concatenate([dk, dv], axis=1)

    def sib_part(b, carry):
        away[b] = part(1 - h, b).astype(bf16)
        return carry

    fold(nb, sib_part, 0)
    pair = copy(away, got, p_sem.at[0], p_sem.at[1], sib)
    pair.start()

    def own_part(i, carry):
        dk = dot(do[i], qa[:rc], NN) * scale
        dv = dot(wo[i], da[:rc], NN)
        both = jnp.concatenate([dk, dv], axis=1).astype(bf16)
        oway[pl.ds(i * zpb, zpb)] = both.reshape(zpb, r_rows, kvw)
        return carry

    fold(no, own_part, 0)

    def back(to, src):
        return copy(oway.at[to], rr.at[src], q_send.at[to], q_recv.at[src], {"seq": to})

    def back_start(i):
        @pl.when(i < z)
        def _():
            back(i, z).start()


    def my_part(b, carry):
        mine[b] = part(h, b)
        return carry

    fold(nb, my_part, 0)
    pair.wait_recv()

    def add(b, carry):
        both = (mine[b] + got[b].astype(f32)).astype(bf16)
        rs[0, pl.ds(b * cpb, cpb)] = both.reshape(cpb, half, kvw)
        return carry

    fold(nb, add, 0)

    def scatter(c, src):
        return copy(rs.at[0, c], rs.at[1, src], s_send.at[c], s_recv.at[src], chip(c))

    loop(1, n, lambda d: scatter((me + d) % n, me).start())
    loop(0, nz, back_start)
    rs[1, me] = rs[0, me]

    def out_own(i, carry):
        o, q = carry
        kv = rk[pl.ds(i * zpb, zpb)].reshape(bo, kvw)
        return o + dot(kv[:, e:], wo[i], TN), q + dot(kv[:, :e], do[i], TN)

    def out_all(i, carry):
        o, q = carry
        kv = pk[pl.ds(i * cpb, cpb)].reshape(bk, kvw)
        return o + dot(kv[:, e:], wp[i], TN), q + dot(kv[:, :e], dp[i], TN)

    zo, za = jnp.zeros((e, rc), f32), jnp.zeros((e, rc + pc), f32)
    o_o, q_o = fold(no, out_own, (zo, zo))
    o_a, q_a = fold(nb2, out_all, (za, za))
    o_r = jnp.transpose(o_a[:, :rc] + o_o)
    o_p = jnp.transpose(o_a[:, rc:])
    q_r = jnp.transpose((q_a[:, :rc] + q_o) * scale)
    q_p = jnp.transpose(q_a[:, rc:] * scale)
    for k in range(r_heads):
        ro[0, :, k * e : (k + 1) * e] = o_r[k * r_rows : (k + 1) * r_rows].astype(bf16)
        rdq[0, :, k * e : (k + 1) * e] = q_r[k * r_rows : (k + 1) * r_rows].astype(bf16)
    for k in range(p_heads):
        po[:, k * e : (k + 1) * e] = o_p[k * rows : (k + 1) * rows].astype(bf16)
        pdq[:, k * e : (k + 1) * e] = q_p[k * rows : (k + 1) * rows].astype(bf16)

    loop(1, n, lambda d: scatter((me + n - d) % n, (me + n - d) % n).wait_recv())
    summed = lax.fori_loop(
        0, n, lambda c, t: t + rs[1, c].astype(f32), jnp.zeros((half, kvw), f32), unroll=min(n, 8)
    )
    fin[h] = summed.astype(bf16)
    last = copy(fin.at[h], fin.at[h], e_sem.at[0], e_sem.at[1], sib)
    last.start()

    def back_wait(i):
        @pl.when(i > z)
        def _():
            back(i, i).wait_recv()

    loop(0, nz, back_wait)
    rr[z] = oway[z]
    own_sum = lax.fori_loop(
        0,
        nz,
        lambda c, t: t + jnp.where(c >= z, rr[c].astype(f32), 0.0),
        jnp.zeros((r_rows, kvw), f32),
        unroll=min(nz, 8),
    )
    rdkv[0] = own_sum.astype(bf16)
    copy(fin.at[1 - h], fin.at[1 - h], e_sem.at[0], e_sem.at[1], sib).wait_recv()
    pdkv[:half, :] = fin[0]
    pdkv[half:, :] = fin[1]

    loop(1, n, lambda d: gather((me + d) % n, me).wait_send())
    loop(1, n, lambda d: pass_on((me + d) % n, h).wait_send())
    loop(1, n, lambda d: scatter((me + d) % n, me).wait_send())

    def sent(i):
        @pl.when(i > z)
        def _():
            resp(i, z).wait_send()

        @pl.when(i < z)
        def _():
            back(i, z).wait_send()

    loop(0, nz, sent)
    pair.wait_send()
    last.wait_send()


def hand_over(*refs):
    sem = refs[-1]
    half = len(refs) // 2
    moves = [pltpu.make_async_copy(refs[k], refs[half + k], sem.at[k]) for k in range(half)]
    for move in moves:
        move.start()
    for move in moves:
        move.wait()


def shards(nz, nx, ns, prompt_q, prompt_kv, prompt_dout, resp_q, resp_kv, resp_dout, resp_lengths):
    n = nz * nx
    rows, kvw = prompt_kv.shape
    e = kvw // 2
    half = rows // 2
    r_rows = resp_q.shape[1]
    rc = resp_q.shape[2] // e * r_rows
    qc = rc + prompt_q.shape[1] // e * rows
    cpb = math.gcd(n, 8)
    bk = cpb * half
    nb2 = 2 * n // cpb
    zpb = math.gcd(nz, 4)
    bo = zpb * r_rows
    no = nz // zpb
    vmem = pl.BlockSpec(memory_space=pltpu.VMEM)
    scratch = [
        ((2 * n, half, kvw), bf16),
        ((nz, r_rows, kvw), bf16),
        ((qc, e), bf16),
        ((qc, e), bf16),
        ((nb2, bk, qc), f32),
        ((nb2, bk, qc), f32 if n <= 32 else bf16),
        ((no, bo, rc), f32),
        ((no, bo, rc), f32),
        ((nb2, bk, qc), bf16),
        ((nb2, bk, qc), bf16),
        ((no, bo, rc), bf16),
        ((no, bo, rc), bf16),
        ((nb2 // 2, bk, kvw), bf16),
        ((nb2 // 2, bk, kvw), bf16),
        ((nb2 // 2, bk, kvw), f32),
        ((2, n, half, kvw), bf16),
        ((nz, r_rows, kvw), bf16),
        ((nz, r_rows, kvw), bf16),
        ((2, half, kvw), bf16),
    ]
    room = sum(math.prod(s) * jnp.dtype(t).itemsize for s, t in scratch)
    dma = pltpu.SemaphoreType.DMA
    heads = qc // rows
    sems = [pltpu.SMEM(resp_lengths.shape, jnp.int32)]
    sems += [dma((k,)) for k in (2 * heads + 4, n, n, n, n, nz, nz, 2, n, n, nz, nz, 2)]
    like = jax.ShapeDtypeStruct
    results = pl.pallas_call(
        functools.partial(kernel, nz, nx, ns),
        out_shape=[
            pltpu.VMEM(a.shape, bf16)
            for a in (prompt_q, resp_q, prompt_q, resp_q, prompt_kv, resp_kv)
        ],
        in_specs=[pl.BlockSpec(memory_space=pltpu.HBM)] * 7,
        out_specs=[vmem] * 6,
        scratch_shapes=[pltpu.VMEM(s, t) for s, t in scratch] + sems,
        compiler_params=pltpu.CompilerParams(
            collective_id=0, has_side_effects=True, vmem_limit_bytes=max(56 * 2**20, room + 3 * 2**20)
        ),
    )(resp_lengths, prompt_q, prompt_kv, prompt_dout, resp_q, resp_kv, resp_dout)
    return pl.pallas_call(
        hand_over,
        out_shape=[like(a.shape, a.dtype) for a in results],
        in_specs=[vmem] * 6,
        out_specs=[pl.BlockSpec(memory_space=pltpu.HBM)] * 6,
        scratch_shapes=[dma((6,))],
        compiler_params=pltpu.CompilerParams(vmem_limit_bytes=4 * 2**20),
    )(*results)


def solution(mesh):
    prompt = P(("grp", "seq", "rep"), "sub")
    prompt_kv = P(("grp", "seq", "rep"), None)
    resp = P(("grp", "rep", "sub"), "seq", None)
    sizes = (mesh.shape["seq"], mesh.shape["rep"], mesh.shape["sub"])
    return jax.shard_map(
        functools.partial(shards, *sizes),
        mesh=mesh,
        in_specs=(prompt, prompt_kv, prompt, resp, resp, resp, P("grp")),
        out_specs=(prompt, resp, prompt, resp, prompt_kv, resp),
        check_vma=False,
    )
```
